256 devices in a mesh: gr: 32 (over z_lo, x, y), gc: 8 (over z_hi, core).
Axes of the slice: x: 4, y: 4, z: 8 (z_hi: 4, z_lo: 2; z = z_hi * 2 + z_lo), core: 2. Of those that a mesh axis runs over, the one named last changes fastest.
Arguments:
- alignment_matrix: bfloat16 [512, 1536, 64], P(('gr', 'gc')), may hold values from -24 to 24
- sequence_validity: int32 [512], replicated, may hold values from 0 to 1, as said below
- residue_validity: int32 [1536], replicated, may hold values 0 or 1
- standardize_gain: float32 [64], replicated, may hold values from 0.1 to 1.9
- standardize_offset: float32 [64], replicated, may hold values from -3 to 3
- first_projector: bfloat16 [64, 32], replicated, may hold values from -0.75 to 0.75
- second_projector: bfloat16 [64, 32], replicated, may hold values from -0.75 to 0.75
- final_projector: bfloat16 [1024, 128], replicated, may hold values from -2 to 2
- final_offset: float32 [128], replicated, may hold values from -3 to 3
Outputs:
- pair_update: bfloat16 [1536, 1536, 128], P('gr', 'gc')
The draws below stay inside these ranges and needn't reach their ends.
Inputs may be any that keep to these rules, and one draw needn't show every extreme that they name: `sequence_validity`: each entry is 0 or 1; the first row is always 1.
All inputs are finite; a program needn't handle non-finite values.
Results may differ from the reference program's by a relative error of at most 0.0052.
Values may be sent and summed in bfloat16 or wider, within the bound.
A program may use at most 128 MiB of HBM per device.

```python
import math
import jax
import jax.numpy as jnp
from jax import lax

ALIGN_FEATURES = 64
HIDDEN_WIDTH = 32
PAIR_FEATURES = 128
SEQUENCE_NUMBER = 512
RESIDUE_NUMBER = 1536


def draw_sequence_validity(key, part):
    key = jax.random.fold_in(key, 11)
    input_entries = jax.random.randint(key, (SEQUENCE_NUMBER,), 0, 4, dtype=jnp.int32)
    present = jnp.minimum(input_entries, 1).astype(jnp.int32)
    return present.at[0].set(1)


def plant(values, stream_key, least, largest):
    longest = values.shape.index(max(values.shape))
    spots = []
    for shift in (0, 1):
        where = [jax.random.randint(jax.random.fold_in(stream_key, axis), (), 0, length) for axis, length in enumerate(values.shape)]
        where[longest] = (where[longest] + shift) % values.shape[longest]
        spots.append(tuple(where))
    return values.at[spots[0]].set(least).at[spots[1]].set(largest)


def with_spikes(values, stream_key, source, target, shards_of, factor):
    owner, partner = [(jnp.arange(values.shape[axis_at]) // (values.shape[axis_at] // shards_of)).reshape([-1 if axis == axis_at else 1 for axis in range(values.ndim)]) for axis_at in (source, target)]
    chosen = jax.random.permutation(stream_key, shards_of)[partner]
    strong = (owner == chosen) | (owner == (partner + shards_of // 2) % shards_of)
    return jnp.where(strong, factor * values, values)


def steps_of(stream_key, dims, split, least, high):
    def one(position, blocks):
        heights = jax.random.uniform(jax.random.fold_in(jax.random.fold_in(stream_key, 6), position), (blocks,), jnp.float32, least / len(split), high / len(split))
        return jnp.repeat(jnp.exp(heights), dims[position] // blocks).reshape((-1,) + (1,) * (len(dims) - position - 1))

    factor_of = one(*split[0])
    for cut in split[1:]:
        factor_of = factor_of * one(*cut)
    return factor_of


def normal_values(own_key, shape, scale, most, pieces=(), kind=jnp.bfloat16):
    level = steps_of(own_key, shape, pieces, -0.22, 0.18) if pieces else 1.0
    entries = jax.random.normal(own_key, shape, jnp.float32) * scale * level
    return jnp.minimum(jnp.maximum(entries, -most), most).astype(kind)


def noise_with(rng, shape, scale, limit, pieces, heavy, kind=jnp.bfloat16):
    values = scale * jax.random.normal(rng, shape, jnp.float32)
    if pieces:
        values = values * steps_of(rng, shape, pieces, -0.22, 0.18)
    return jnp.clip(with_spikes(values, jax.random.fold_in(rng, 3), *heavy), -limit, limit).astype(kind)


def setup_inputs(seed: int = 0) -> dict:
    keys = jax.random.split(jax.random.key(seed), 10)
    return {
        "alignment_matrix": noise_with(keys[0], (SEQUENCE_NUMBER, RESIDUE_NUMBER, ALIGN_FEATURES), 1.0, 24.0, ((0, 256),), (0, 1, 256, 6.0)),
        "sequence_validity": draw_sequence_validity(jax.random.fold_in(keys[9], 71), 0),
        "residue_validity": plant((jax.random.randint(keys[2], (RESIDUE_NUMBER,), 0, 8) < 7).astype(jnp.int32), jax.random.fold_in(keys[2], 1), 0, 1),
        "standardize_gain": jnp.clip(1.0 + 0.18 * jax.random.normal(keys[3], (ALIGN_FEATURES,), jnp.float32), 0.1, 1.9),
        "standardize_offset": normal_values(keys[4], (ALIGN_FEATURES,), 0.5, 3.0, (), jnp.float32),
        "first_projector": normal_values(keys[5], (ALIGN_FEATURES, HIDDEN_WIDTH), ALIGN_FEATURES ** -0.5, 0.75),
        "second_projector": normal_values(keys[6], (ALIGN_FEATURES, HIDDEN_WIDTH), ALIGN_FEATURES ** -0.5, 0.75),
        "final_projector": normal_values(keys[7], (HIDDEN_WIDTH * HIDDEN_WIDTH, PAIR_FEATURES), (max(HIDDEN_WIDTH * HIDDEN_WIDTH * 4 // SEQUENCE_NUMBER, 1)) ** -0.5, 2.0),
        "final_offset": normal_values(keys[8], (PAIR_FEATURES,), 0.5, 3.0, (), jnp.float32),
    }


def standardize_features(input_entries, gain, shift):
    input_entries = input_entries.astype(jnp.float32)
    center = lax.optimization_barrier(jnp.mean(input_entries, axis=-1, keepdims=True))
    spread = lax.optimization_barrier(jnp.mean((input_entries - center) ** 2, axis=-1, keepdims=True))
    return (input_entries - center) * lax.rsqrt(spread + 1e-05) * gain + shift

def reference(alignment_matrix, sequence_validity, residue_validity, standardize_gain, standardize_offset, first_projector, second_projector, final_projector, final_offset):
    standardized_alignment = standardize_features(alignment_matrix, standardize_gain, standardize_offset).astype(jnp.bfloat16).astype(jnp.float32)
    retained_flags = sequence_validity.astype(jnp.float32)[:, None, None] * residue_validity.astype(jnp.float32)[None, :, None]
    first_factor = jnp.einsum('qwg,gk->qwk', standardized_alignment, first_projector.astype(jnp.float32), precision=lax.Precision.HIGHEST)
    first_factor = (first_factor * retained_flags).astype(jnp.bfloat16).astype(jnp.float32)
    second_factor = jnp.einsum('qwg,gk->qwk', standardized_alignment, second_projector.astype(jnp.float32), precision=lax.Precision.HIGHEST)
    second_factor = (second_factor * retained_flags).astype(jnp.bfloat16).astype(jnp.float32)
    divisor_sum = jnp.sum(sequence_validity.astype(jnp.float32))
    weight3 = final_projector.astype(jnp.float32).reshape(HIDDEN_WIDTH, HIDDEN_WIDTH, PAIR_FEATURES)
    block = math.gcd(RESIDUE_NUMBER, 48)
    nblocks = RESIDUE_NUMBER // block

    def one_block(index):
        lefts = lax.dynamic_slice_in_dim(first_factor, index * block, block, 1)
        outer = jnp.einsum('sic,sjd->icjd', lefts, second_factor, precision=lax.Precision.HIGHEST)
        outer = lax.optimization_barrier(outer.astype(jnp.bfloat16)).astype(jnp.float32)
        projected = jnp.einsum('icjd,cdz->ijz', outer, weight3, precision=lax.Precision.HIGHEST)
        return (projected / divisor_sum + final_offset).astype(jnp.bfloat16)
    result = lax.map(one_block, jnp.arange(nblocks, dtype=jnp.int32))
    return result.reshape(RESIDUE_NUMBER, RESIDUE_NUMBER, PAIR_FEATURES)
```

```python
import functools
import jax
import jax.numpy as jnp
from jax import lax
from jax.experimental import pallas as pl
from jax.experimental.pallas import tpu as pltpu
from jax.sharding import PartitionSpec as P

F32 = jnp.float32
BF16 = jnp.bfloat16
MESH = pl.DeviceIdType.MESH
NT = (((1,), (1,)), ((), ()))


def iota(shape, dim):
    return lax.broadcasted_iota(jnp.int32, shape, dim)


def ones_where(cond):
    return jnp.where(cond, 1.0, 0.0).astype(BF16)


def dot(a, b):
    return jnp.dot(a, b, preferred_element_type=F32)


def dot_nt(a, b):
    return lax.dot_general(a, b, NT, preferred_element_type=F32)


def where_am_i():
    gr = lax.axis_index("gr")
    gc = lax.axis_index("gc")
    zl = gr // 16
    pos = gr % 16
    zc = ((gc // 2) * 2 + zl) * 2 + gc % 2
    return gr, gc, zl, pos, zc


def ring_device(zl_to_gr, zc):
    z = zc // 2
    return {"gr": (z % 2) * 16 + zl_to_gr, "gc": (z // 2) * 2 + zc % 2}


def plane_device(zl, gc, pos):
    return {"gr": zl * 16 + pos, "gc": gc}


def comm_kernel(
    sv_smem, msa_ref, rv_ref, gain_ref, off_ref, w1_ref, w2_ref,
    rg, lg,
    rs, rb, ls, la, lb, nf, lq, lsf, gainv,
    rs_send, rs_recv, ls_send, ls_recv, lz_send, lz_recv, lt_send, lt_recv,
    g_send, g_recv,
):
    gr, gc, zl, pos, zc = where_am_i()
    core = gc % 2
    px, py = pos // 4, pos % 4

    barrier = pltpu.get_barrier_semaphore()

    @pl.loop(1, 16)
    def _(o):
        pl.semaphore_signal(barrier, inc=1, device_id=ring_device(pos, (zc + o) % 16), device_id_type=MESH)
        pl.semaphore_signal(barrier, inc=1, device_id=plane_device(zl, gc, (pos + o) % 16), device_id_type=MESH)

    k = iota((64, 128), 0)
    lane = iota((64, 128), 1)
    both = [
        jnp.where(lane // 64 == r, jnp.where(lane % 64 == k, 1.0, 0.0) - 1.0 / 64, 0.0).astype(BF16)
        for r in range(2)
    ]
    mean2 = jnp.where(iota((128, 128), 0) // 64 == iota((128, 128), 1) // 64, 1.0 / 64, 0.0).astype(BF16)
    t1 = ones_where(iota((512, 64), 0) % 64 == iota((512, 64), 1))
    t2 = ones_where(iota((32, 256), 1) % 32 == iota((32, 256), 0))
    row, col = iota((512, 256), 0), iota((512, 256), 1)
    wl = dot(dot(t1, w1_ref[...]).astype(BF16), t2)
    wl = jnp.where((row // 128 == (col // 32) % 4) & ((row // 64) % 2 == col // 128), wl, 0.0).astype(BF16)
    t3 = ones_where(iota((64, 32), 0) % 32 == iota((64, 32), 1))
    t4 = ones_where(iota((64, 128), 1) % 64 == iota((64, 128), 0))
    wr = dot(dot_nt(t3, w2_ref[...]).astype(BF16), t4)
    wr = jnp.where(iota((64, 128), 0) // 32 == iota((64, 128), 1) // 64, wr, 0.0).astype(BF16)
    gainv[0:1, 0:64] = gain_ref[...]
    gainv[0:1, 64:128] = gain_ref[...]
    gainv[1:2, 0:64] = off_ref[...]
    gainv[1:2, 64:128] = off_ref[...]
    sv0 = sv_smem[(gr * 8 + gc) * 2].astype(F32)
    sv1 = sv_smem[(gr * 8 + gc) * 2 + 1].astype(F32)
    svm = jnp.where(iota((64, 384), 0) < 32, sv0, sv1)
    low = iota((16, 128), 1) < 64

    @pl.loop(0, 4)
    def _(g):
        rows = pl.ds(pl.multiple_of(g * 384, 384), 384)
        d = dot(msa_ref[0, rows, :], both[0]) + dot(msa_ref[1, rows, :], both[1])
        dd = d * d
        hi = dd.astype(BF16)
        lo = (dd - hi.astype(F32)).astype(BF16)
        var = dot(hi, mean2) + dot(lo, mean2)
        n = (d * lax.rsqrt(var + 1e-05) * gainv[0:1, :] + gainv[1:2, :]).astype(BF16)
        nf[rows, :] = n.astype(F32)
        y = dot_nt(wr, n) * svm * rv_ref[g].astype(F32)
        for r in range(2):
            yr = y[r * 32 : r * 32 + 32]
            a, b = yr[0:16, 128:256], yr[16:32, 128:256]
            rs[2 * g, 0, r] = yr[0:16, 0:128].astype(BF16)
            rs[2 * g, 1, r] = yr[16:32, 0:128].astype(BF16)
            rs[2 * g, 2, r] = jnp.where(low, a, pltpu.roll(b, 64, axis=1)).astype(BF16)
            rs[2 * g + 1, 0, r] = yr[0:16, 256:384].astype(BF16)
            rs[2 * g + 1, 1, r] = yr[16:32, 256:384].astype(BF16)
            rs[2 * g + 1, 2, r] = jnp.where(low, pltpu.roll(a, 64, axis=1), b).astype(BF16)

    x4 = jnp.concatenate([nf[pl.ds(m, 384, stride=4), :] for m in range(4)], axis=1).astype(BF16)
    left = dot(x4, wl)
    lq[0] = left[:, 0:128]
    lq[1] = left[:, 128:256]
    for p in range(16):
        for l in range(2):
            for r in range(2):
                at = 12 * (l * 16 + p)
                lsf[p, l * 24 + r * 12 : l * 24 + r * 12 + 12, :] = lq[r, at : at + 12, :]
    ls[...] = lsf[...].astype(BF16)

    pl.semaphore_wait(barrier, 30)

    def rs_copy(p, o):
        to = (zc + o) % 16
        dev = ring_device(pos, to)
        return pltpu.make_async_remote_copy(
            src_ref=rs.at[dev["gc"], p], dst_ref=rb.at[p, zc],
            send_sem=rs_send.at[p, o], recv_sem=rs_recv.at[p, o],
            device_id=dev, device_id_type=MESH)

    def rs_wait(p, o):
        frm = (zc - o + 16) % 16
        return pltpu.make_async_remote_copy(
            src_ref=rs.at[0, p], dst_ref=rb.at[p, frm],
            send_sem=rs_send.at[p, o], recv_sem=rs_recv.at[p, o],
            device_id=ring_device(pos, frm), device_id_type=MESH)

    def ls_copy(o):
        to = (pos + o) % 16
        return pltpu.make_async_remote_copy(
            src_ref=ls.at[to], dst_ref=la.at[pos],
            send_sem=ls_send.at[o], recv_sem=ls_recv.at[o],
            device_id=plane_device(zl, gc, to), device_id_type=MESH)

    def ls_wait(o):
        frm = (pos - o + 16) % 16
        return pltpu.make_async_remote_copy(
            src_ref=ls.at[0], dst_ref=la.at[frm],
            send_sem=ls_send.at[o], recv_sem=ls_recv.at[o],
            device_id=plane_device(zl, gc, frm), device_id_type=MESH)

    @pl.loop(1, 16)
    def _(o):
        rs_copy(0, o).start()

    @pl.loop(1, 16)
    def _(o):
        ls_copy(o).start()

    for p in range(1, 3):

        @pl.loop(1, 16)
        def _(o, p=p):
            rs_copy(p, o).start()

    for p in range(3):
        rb[p, zc] = rs[gc, p]
    la[pos] = ls[pos]

    def flat(x, y):
        return ((x + 4) % 4) * 4 + (y + 4) % 4

    def along(half, a, b):
        return flat(px + a, py + b) if half == 0 else flat(px + b, py + a)

    def g_copy(p, half, sem, who, part, da, db):
        t0, tn = {"all": (0, 8), "lo": (0, 4), "hi": (4, 4)}[part]
        t = pl.ds(16 * p + 8 * half + t0, tn)
        return pltpu.make_async_remote_copy(
            src_ref=rg.at[who, t], dst_ref=rg.at[who, t],
            send_sem=g_send.at[p, half, sem], recv_sem=g_recv.at[p, half, sem],
            device_id=plane_device(zl, gc, along(half, da, db)), device_id_type=MESH)

    sent = []

    def send(*args):
        c = g_copy(*args)
        c.start()
        sent.append(c)

    def stage1_start(p, half):
        me = along(half, 0, 0)
        send(p, half, 0, me, "all", 1, 0)
        send(p, half, 1, me, "all", -1, 0)

    def stage1_forward(p, half):
        g_copy(p, half, 0, along(half, -1, 0), "all", 1, 0).wait_recv()
        send(p, half, 2, along(half, -1, 0), "lo", 1, 0)
        g_copy(p, half, 1, along(half, 1, 0), "all", -1, 0).wait_recv()
        send(p, half, 3, along(half, 1, 0), "hi", -1, 0)

    def stage1_end(p, half):
        g_copy(p, half, 2, along(half, 2, 0), "lo", 1, 0).wait_recv()
        g_copy(p, half, 3, along(half, 2, 0), "hi", -1, 0).wait_recv()

    shifts = (0, -1, 1, 2)

    def stage2_start(p, half, u):
        s = 4 + 4 * u
        who = along(half, shifts[u], 0)
        send(p, half, s, who, "all", 0, 1)
        send(p, half, s + 1, who, "all", 0, -1)

    def stage2_forward(p, half, u):
        s = 4 + 4 * u
        minus, plus = along(half, shifts[u], -1), along(half, shifts[u], 1)
        g_copy(p, half, s, minus, "all", 0, 1).wait_recv()
        send(p, half, s + 2, minus, "lo", 0, 1)
        g_copy(p, half, s + 1, plus, "all", 0, -1).wait_recv()
        send(p, half, s + 3, plus, "hi", 0, -1)

    def stage2_end(p, half, u):
        s = 4 + 4 * u
        g_copy(p, half, s + 2, along(half, shifts[u], 2), "lo", 0, 1).wait_recv()
        g_copy(p, half, s + 3, along(half, shifts[u], 2), "hi", 0, -1).wait_recv()

    o0, i0 = iota((512, 1), 0), iota((512, 512), 1)
    perm0 = ones_where((o0 % 32) * 16 + o0 // 32 == i0)

    def assemble_right(p):
        @pl.loop(1, 16)
        def _(o):
            rs_wait(p, o).wait_recv()

        x = rb[p].reshape(512, 128)
        rg[pos, 16 * p : 16 * p + 16] = dot(perm0, x).astype(BF16).reshape(16, 32, 128)

    def assemble_left():
        @pl.loop(1, 16)
        def _(o):
            ls_wait(o).wait_recv()

        o1, i1 = iota((768, 1), 0), iota((768, 768), 1)
        lq1 = o1 // 32
        l1 = jnp.where(lq1 >= 12, 1, 0)
        at = ((o1 // 2) % 16) * 48 + l1 * 24 + (o1 % 2) * 12 + (lq1 - 12 * l1)
        perm1 = ones_where(at == i1)
        y = dot(perm1, la[...].reshape(768, 128)).astype(BF16)
        lb[...] = y.reshape(2, 12, 32, 128)
        lg[zc] = lb[zl]

    def lz_copy(o):
        to = (zc + 2 * o) % 16
        return pltpu.make_async_remote_copy(
            src_ref=lb.at[(to // 2) % 2], dst_ref=lg.at[zc],
            send_sem=lz_send.at[o], recv_sem=lz_recv.at[o],
            device_id=ring_device(pos, to), device_id_type=MESH)

    def lz_wait(o):
        frm = (zc - 2 * o + 16) % 16
        return pltpu.make_async_remote_copy(
            src_ref=lb.at[0], dst_ref=lg.at[frm],
            send_sem=lz_send.at[o], recv_sem=lz_recv.at[o],
            device_id=ring_device(pos, frm), device_id_type=MESH)

    twin = {"gr": gr, "gc": gc + 1 - 2 * core}

    def lt_copy(o):
        frm = (zc - 2 * o + 16) % 16
        return pltpu.make_async_remote_copy(
            src_ref=lg.at[frm], dst_ref=lg.at[frm],
            send_sem=lt_send.at[o], recv_sem=lt_recv.at[o],
            device_id=twin, device_id_type=MESH)

    def lt_wait(o):
        frm = (zc + 1 - 2 * core - 2 * o + 16) % 16
        return pltpu.make_async_remote_copy(
            src_ref=lg.at[frm], dst_ref=lg.at[frm],
            send_sem=lt_send.at[o], recv_sem=lt_recv.at[o],
            device_id=twin, device_id_type=MESH)

    assemble_right(0)
    for h in range(2):
        stage1_start(0, h)
    assemble_left()

    @pl.loop(1, 8)
    def _(o):
        lz_copy(o).start()

    lt_copy(0).start()
    for h in range(2):
        stage1_forward(0, h)
        stage2_start(0, h, 0)
    for h in range(2):
        for u in (1, 2):
            stage2_start(0, h, u)
    assemble_right(1)
    for h in range(2):
        stage1_start(1, h)
    assemble_right(2)
    for h in range(2):
        stage1_end(0, h)
        stage2_start(0, h, 3)
    for p in range(3):
        for h in range(2):
            stage2_forward(p, h, 0)
        if p < 2:
            for h in range(2):
                stage1_forward(p + 1, h)
                for u in range(3):
                    stage2_start(p + 1, h, u)
            if p < 1:
                for h in range(2):
                    stage1_start(2, h)
        for u in (1, 2, 3):
            for h in range(2):
                stage2_forward(p, h, u)
        if p < 2:
            for h in range(2):
                stage1_end(p + 1, h)
                stage2_start(p + 1, h, 3)
        for u in range(4):
            for h in range(2):
                stage2_end(p, h, u)
        if p == 0:

            @pl.loop(1, 8)
            def _(o):
                lz_wait(o).wait_recv()
                lt_copy(o).start()

    @pl.loop(0, 8)
    def _(o):
        lt_wait(o).wait_recv()

    for c in sent:
        c.wait_send()

    @pl.loop(1, 16)
    def _(o):
        ls_copy(o).wait_send()
        for p in range(3):
            rs_copy(p, o).wait_send()

    @pl.loop(1, 8)
    def _(o):
        lz_copy(o).wait_send()

    @pl.loop(0, 8)
    def _(o):
        lt_copy(o).wait_send()


def tile_kernel(
    rv_smem, sv_ref, rg, lg, fp_ref, off_ref,
    out_ref,
    fpf, wd, wt, lt, outer, acc,
):
    gr = lax.axis_index("gr")
    core = lax.axis_index("gc") % 2
    eye = ones_where(iota((128, 128), 0) == iota((128, 128), 1))
    fpf[...] = fp_ref[...].astype(F32)
    for d in range(32):
        wd[32 * d : 32 * d + 32, :] = fpf[pl.ds(d, 32, stride=32), :].astype(BF16)
    wfull = dot_nt(eye, wd[...]).astype(BF16)
    wt[0:128, :] = wfull[:, 0:512]
    wt[128:256, :] = wfull[:, 512:1024]
    o2, i2 = iota((512, 1), 0), iota((512, 512), 1)
    perm2 = ones_where(((o2 // 2) % 16) * 32 + (o2 // 32) * 2 + o2 % 2 == i2)

    @pl.loop(0, 12)
    def _(q):
        y = dot(perm2, lg[:, q].reshape(512, 128)).astype(BF16)
        lt[pl.ds(pl.multiple_of(q * 128, 128), 128), :] = dot_nt(eye, y).astype(BF16)

    count = jnp.sum(sv_ref[...].astype(F32))
    inv = 1.0 / jnp.full((1, 128), count, F32)
    off_a = pl.multiple_of(64 * core, 64)
    off_b = pl.multiple_of(128 - 128 * core, 64)

    for p in range(3):

        @pl.loop(0, 6)
        def _(ib, p=p):
            x = lt[pl.ds(pl.multiple_of(ib * 256, 256), 256), :]
            for t in range(0, 16, 2):
                w = jnp.concatenate(
                    [rg[:, 16 * p + t + e].reshape(512, 128) for e in range(2)], axis=1)
                s = dot(x, w).astype(BF16)
                for i in range(8):
                    for e in range(2):
                        outer[i, t + e] = s[i * 32 : i * 32 + 32, e * 128 : e * 128 + 128]
            for i in range(0, 8, 2):
                w = jnp.concatenate([outer[i + e].reshape(512, 128) for e in range(2)], axis=1)
                if p == 0:
                    y = dot(wt[0:128, :], w)
                    for e in range(2):
                        acc[ib * 8 + i + e] = y[:, e * 128 : e * 128 + 128]
                elif p == 1:
                    y = dot(wt[128:256, :], w)
                    for e in range(2):
                        acc[ib * 8 + i + e] = acc[ib * 8 + i + e] + y[:, e * 128 : e * 128 + 128]
                else:
                    y = dot(wt[...], w)
                    for e in range(2):
                        at = ib * 8 + i + e
                        scale = inv * rv_smem[gr * 48 + at].astype(F32)
                        ya = acc[at].T * scale + off_ref[...]
                        yb = (y[0:128, e * 128 : e * 128 + 128].T[0:64]
                              + y[128:256, e * 128 : e * 128 + 128].T[64:128])
                        yb = yb * scale + off_ref[...]
                        out_ref[at, pl.ds(off_a, 128), :] = ya.astype(BF16)
                        out_ref[at, pl.ds(off_b, 64), :] = yb.astype(BF16)


def vmem():
    return pl.BlockSpec(memory_space=pltpu.VMEM)


def smem():
    return pl.BlockSpec(memory_space=pltpu.SMEM)


def on_device(msa, sv, rv, gain, offset, w1, w2, wz, bz):
    dma = pltpu.SemaphoreType.DMA
    rg, lg = pl.pallas_call(
        comm_kernel,
        out_shape=(
            jax.ShapeDtypeStruct((16, 48, 32, 128), BF16),
            jax.ShapeDtypeStruct((16, 12, 32, 128), BF16),
        ),
        in_specs=[smem()] + [vmem()] * 6,
        out_specs=(vmem(), vmem()),
        scratch_shapes=[
            pltpu.VMEM((8, 3, 2, 16, 128), BF16),
            pltpu.VMEM((3, 16, 2, 16, 128), BF16),
            pltpu.VMEM((16, 48, 128), BF16),
            pltpu.VMEM((16, 48, 128), BF16),
            pltpu.VMEM((2, 12, 32, 128), BF16),
            pltpu.VMEM((1536, 128), F32),
            pltpu.VMEM((2, 384, 128), F32),
            pltpu.VMEM((16, 48, 128), F32),
            pltpu.VMEM((8, 128), F32),
            dma((3, 16)), dma((3, 16)),
            dma((16,)), dma((16,)),
            dma((8,)), dma((8,)),
            dma((8,)), dma((8,)),
            dma((3, 2, 20)), dma((3, 2, 20)),
        ],
        compiler_params=pltpu.CompilerParams(
            collective_id=0, has_side_effects=True, vmem_limit_bytes=40 * 2**20),
    )(sv, msa, rv.reshape(4, 1, 384), gain.reshape(1, 64), offset.reshape(1, 64), w1, w2)
    return pl.pallas_call(
        tile_kernel,
        out_shape=jax.ShapeDtypeStruct((48, 192, 128), BF16),
        in_specs=[smem()] + [vmem()] * 5,
        out_specs=vmem(),
        scratch_shapes=[
            pltpu.VMEM((1024, 128), F32),
            pltpu.VMEM((1024, 128), BF16),
            pltpu.VMEM((256, 512), BF16),
            pltpu.VMEM((1536, 512), BF16),
            pltpu.VMEM((8, 16, 32, 128), BF16),
            pltpu.VMEM((48, 128, 128), F32),
        ],
        compiler_params=pltpu.CompilerParams(vmem_limit_bytes=40 * 2**20),
        cost_estimate=pl.CostEstimate(flops=12 * 10**9, bytes_accessed=10**7, transcendentals=0),
    )(rv, sv.reshape(4, 128), rg, lg, wz, bz.reshape(1, 128))


def solution(mesh):
    in_specs = (P(("gr", "gc"), None, None), P(), P(), P(), P(), P(), P(), P(), P())
    out_specs = P("gr", "gc", None)
    return jax.shard_map(
        on_device, mesh=mesh, in_specs=in_specs, out_specs=out_specs, check_vma=False
    )
```

```python
import functools
import jax
import jax.numpy as jnp
from jax import lax
from jax.experimental import pallas as pl
from jax.experimental.pallas import tpu as pltpu
from jax.sharding import PartitionSpec as P

F32 = jnp.float32
BF16 = jnp.bfloat16
MESH = pl.DeviceIdType.MESH
NT = (((1,), (1,)), ((), ()))


def iota(shape, dim):
    return lax.broadcasted_iota(jnp.int32, shape, dim)


def ones_where(cond):
    return jnp.where(cond, 1.0, 0.0).astype(BF16)


def dot(a, b):
    return jnp.dot(a, b, preferred_element_type=F32)


def dot_nt(a, b):
    return lax.dot_general(a, b, NT, preferred_element_type=F32)


def where_am_i():
    gr = lax.axis_index("gr")
    gc = lax.axis_index("gc")
    zl = gr // 16
    pos = gr % 16
    zc = ((gc // 2) * 2 + zl) * 2 + gc % 2
    return gr, gc, zl, pos, zc


def ring_device(zl_to_gr, zc):
    z = zc // 2
    return {"gr": (z % 2) * 16 + zl_to_gr, "gc": (z // 2) * 2 + zc % 2}


def plane_device(zl, gc, pos):
    return {"gr": zl * 16 + pos, "gc": gc}


PIECES = (32, 40, 0, 8, 16, 24)
TILES = 8


def first_product(lt, rg, outer, ib, t0):
    x = lt[pl.ds(pl.multiple_of(ib * 512, 512), 512), :]
    for t in range(0, TILES, 2):
        w = jnp.concatenate([rg[:, t0 + t + e].reshape(512, 128) for e in range(2)], axis=1)
        s = dot(x, w).astype(BF16)
        for i in range(16):
            for e in range(2):
                outer[i, t + e] = s[i * 32 : i * 32 + 32, e * 128 : e * 128 + 128]


def second_product(w, outer, i):
    return dot(w, jnp.concatenate([outer[i + e].reshape(TILES * 32, 128) for e in range(2)], axis=1))


def main_kernel(
    sv_hbm, sv4_hbm, rv_hbm, rv12_hbm, msa_hbm, gain_hbm, off_hbm, w1_hbm, w2_hbm, wz_hbm, bz_hbm,
    out_hbm,
    rg, lt, acc, accb, outv, scale, wt, bz,
    sv_smem, rv_smem, sv4, rv12, msa, gain1, off1, w1, w2, wz,
    rs, rb, ls, la, lb, lg, n2, x4, lq, lsf, gainv, fpf, wd, outer,
    in_sem, out_sem, rs_send, rs_recv, ls_send, ls_recv, lz_send, lz_recv, lt_send, lt_recv,
    g_send, g_recv,
):
    gr, gc, zl, pos, zc = where_am_i()
    core = gc % 2
    px, py = pos // 4, pos % 4
    twin = {"gr": gr, "gc": gc + 1 - 2 * core}

    moves = [
        pltpu.make_async_copy(src, dst, in_sem.at[i])
        for i, (src, dst) in enumerate((
            (msa_hbm, msa), (gain_hbm, gain1), (off_hbm, off1), (w2_hbm, w2), (rv12_hbm, rv12), (sv_hbm, sv_smem),
            (w1_hbm, w1), (sv4_hbm, sv4), (rv_hbm, rv_smem), (wz_hbm, wz), (bz_hbm, bz)))
    ]
    for m in moves:
        m.start()

    barrier = pltpu.get_barrier_semaphore()

    @pl.loop(1, 16)
    def _(o):
        pl.semaphore_signal(barrier, inc=1, device_id=ring_device(pos, (zc + o) % 16), device_id_type=MESH)
        pl.semaphore_signal(barrier, inc=1, device_id=plane_device(zl, gc, (pos + o) % 16), device_id_type=MESH)

    for m in moves[:6]:
        m.wait()

    gainv[0:1, 0:64] = gain1[...]
    gainv[0:1, 64:128] = gain1[...]
    gainv[1:2, 0:64] = off1[...]
    gainv[1:2, 64:128] = off1[...]
    gcol = jnp.broadcast_to(gainv[0:1, :], (128, 128)).T[0:64]
    ocol = jnp.broadcast_to(gainv[1:2, :], (128, 128)).T[0:64]
    gcol = jnp.concatenate([gcol] * 3, axis=1)
    ocol = jnp.concatenate([ocol] * 3, axis=1)
    low = iota((16, 128), 1) < 64
    for g in range(4):
        present = jnp.concatenate([rv12[3 * g + k : 3 * g + k + 1, :] for k in range(3)], axis=1).astype(F32)
        for r in range(2):
            x = msa[r, :, 384 * g : 384 * g + 384].astype(F32)
            d = x - jnp.mean(x, axis=0, keepdims=True)
            var = jnp.mean(d * d, axis=0, keepdims=True)
            n = (d * lax.rsqrt(var + 1e-05) * gcol + ocol).astype(BF16)
            n2[r * 64 : r * 64 + 64, 384 * g : 384 * g + 384] = n
            yr = dot(w2[...], n) * (present * sv_smem[(gr * 8 + gc) * 2 + r].astype(F32))
            a, b = yr[0:16, 128:256], yr[16:32, 128:256]
            rs[2 * g, 0, r] = jnp.where(low, a, pltpu.roll(b, 64, axis=1)).astype(BF16)
            rs[2 * g, 1, r] = yr[0:16, 0:128].astype(BF16)
            rs[2 * g, 2, r] = yr[16:32, 0:128].astype(BF16)
            rs[2 * g + 1, 0, r] = jnp.where(low, pltpu.roll(a, 64, axis=1), b).astype(BF16)
            rs[2 * g + 1, 1, r] = yr[0:16, 256:384].astype(BF16)
            rs[2 * g + 1, 2, r] = yr[16:32, 256:384].astype(BF16)

    pl.semaphore_wait(barrier, 30)

    def wait_bytes(ref, sem):
        pltpu.make_async_copy(ref, ref, sem).wait()

    def rs_start(first, n):
        part = pl.ds(first, n)

        @pl.loop(1, 16)
        def _(o):
            to = ring_device(pos, (zc + o) % 16)
            pltpu.make_async_remote_copy(
                src_ref=rs.at[to["gc"], part], dst_ref=rb.at[part, zc],
                send_sem=rs_send, recv_sem=rs_recv.at[first],
                device_id=to, device_id_type=MESH).start()

        for p in range(first, first + n):
            rb[p, zc] = rs[gc, p]

    rs_start(0, 1)
    rs_start(1, 2)

    for m in moves[6:]:
        m.wait()
    sel = ones_where((iota((128, 128), 0) % 32) * 4 + iota((128, 128), 0) // 32 == iota((128, 128), 1))
    for k in range(12):
        t = dot_nt(sel, n2[:, 128 * k : 128 * k + 128]).astype(BF16)
        for m in range(4):
            x4[32 * k : 32 * k + 32, 128 * m : 128 * m + 128] = t[32 * m : 32 * m + 32]
    t1 = ones_where(iota((512, 64), 0) % 64 == iota((512, 64), 1))
    t2 = ones_where(iota((32, 256), 1) % 32 == iota((32, 256), 0))
    row, col = iota((512, 256), 0), iota((512, 256), 1)
    wl = dot(dot_nt(t1, w1[...]).astype(BF16), t2)
    wl = jnp.where((row // 128 == (col // 32) % 4) & ((row // 64) % 2 == col // 128), wl, 0.0).astype(BF16)
    left = dot(x4[...], wl)
    lq[0] = left[:, 0:128]
    lq[1] = left[:, 128:256]
    for p in range(16):
        for l in range(2):
            for r in range(2):
                at = 12 * (l * 16 + p)
                lsf[p, l * 24 + r * 12 : l * 24 + r * 12 + 12, :] = lq[r, at : at + 12, :]
    ls[...] = lsf[...].astype(BF16)

    @pl.loop(1, 16)
    def _(o):
        to = (pos + o) % 16
        pltpu.make_async_remote_copy(
            src_ref=ls.at[to], dst_ref=la.at[pos],
            send_sem=ls_send, recv_sem=ls_recv,
            device_id=plane_device(zl, gc, to), device_id_type=MESH).start()

    la[pos] = ls[pos]

    def flat(x, y):
        return ((x + 4) % 4) * 4 + (y + 4) % 4

    def along(half, a, b):
        return flat(px + a, py + b) if half == 0 else flat(px + b, py + a)

    def g_send_to(k, half, level, who, part, da, db):
        t0, unit = PIECES[k], TILES // 2
        u0, un = {"all": (0, unit), "lo": (0, unit // 2), "hi": (unit // 2, unit // 2)}[part]
        t = pl.ds(t0 + unit * half + u0, un)
        pltpu.make_async_remote_copy(
            src_ref=rg.at[who, t], dst_ref=rg.at[who, t],
            send_sem=g_send, recv_sem=g_recv.at[k, level - 1],
            device_id=plane_device(zl, gc, along(half, da, db)), device_id_type=MESH).start()

    def both_ways(k, level, u):
        for h in range(2):
            g_send_to(k, h, level, along(h, u, 0), "all", 0, 1)
            g_send_to(k, h, level, along(h, u, 0), "all", 0, -1)

    def forward(k, u):
        for h in range(2):
            g_send_to(k, h, 4, along(h, u, -1), "lo", 0, 1)
            g_send_to(k, h, 4, along(h, u, 1), "hi", 0, -1)

    def level0(k):
        for h in range(2):
            g_send_to(k, h, 1, along(h, 0, 0), "all", 1, 0)
            g_send_to(k, h, 1, along(h, 0, 0), "all", -1, 0)
        both_ways(k, 1, 0)

    def level1(k):
        wait_bytes(rg.at[0:8, 0 : TILES // 2], g_recv.at[k, 0])
        for h in range(2):
            g_send_to(k, h, 2, along(h, -1, 0), "lo", 1, 0)
            g_send_to(k, h, 2, along(h, 1, 0), "hi", -1, 0)
        both_ways(k, 2, 3)
        both_ways(k, 2, 1)
        forward(k, 0)

    def level2(k):
        wait_bytes(rg.at[0:10, 0 : TILES // 2], g_recv.at[k, 1])
        both_ways(k, 3, 2)
        forward(k, 3)
        forward(k, 1)

    def level3(k):
        wait_bytes(rg.at[0:4, 0 : TILES // 2], g_recv.at[k, 2])
        forward(k, 2)

    def level4(k):
        wait_bytes(rg.at[0:8, 0 : TILES // 2], g_recv.at[k, 3])

    levels = (level0, level1, level2, level3, level4)

    def wave(i):
        for d in range(4, -1, -1):
            for k, first in enumerate((0, 0, 1, 2, 3, 4)):
                if first + d == i:
                    levels[d](k)

    o0, i0 = iota((512, 1), 0), iota((512, 512), 1)
    perm0 = ones_where((o0 % 32) * 16 + o0 // 32 == i0)

    def assemble_right(p):
        x = rb[p].reshape(512, 128)
        t0 = (32, 0, 16)[p]
        rg[pos, t0 : t0 + 16] = dot(perm0, x).astype(BF16).reshape(16, 32, 128)

    def assemble_left():
        o1, i1 = iota((768, 1), 0), iota((768, 768), 1)
        lq1 = o1 // 32
        l1 = jnp.where(lq1 >= 12, 1, 0)
        at = ((o1 // 2) % 16) * 48 + l1 * 24 + (o1 % 2) * 12 + (lq1 - 12 * l1)
        perm1 = ones_where(at == i1)

        wait_bytes(la.at[0:15], ls_recv)
        y = dot(perm1, la[...].reshape(768, 128)).astype(BF16)
        lb[...] = y.reshape(2, 12, 32, 128)
        lg[zc] = lb[zl]

    def at_z(d):
        return (zc + 2 * d + 16) % 16

    def lz(level, src, slot, to, part):
        t = pl.ds(*{"all": (0, 12), "lo": (0, 6), "hi": (6, 6)}[part])
        pltpu.make_async_remote_copy(
            src_ref=src.at[t], dst_ref=lg.at[slot, t],
            send_sem=lz_send, recv_sem=lz_recv.at[level],
            device_id=ring_device(pos, at_z(to)), device_id_type=MESH).start()

    def twin_send(d):
        pltpu.make_async_remote_copy(
            src_ref=lg.at[at_z(d)], dst_ref=lg.at[at_z(d)],
            send_sem=lt_send, recv_sem=lt_recv,
            device_id=twin, device_id_type=MESH).start()

    def lz_start():
        for d in (1, -1):
            lz(0, lb.at[1 - zl], zc, d, "all")
        for d in (2, -2):
            lz(0, lb.at[zl], zc, d, "all")
        twin_send(0)

    def lz_forward():
        wait_bytes(lg.at[0:4], lz_recv.at[0])
        for d in (1, -1):
            lz(1, lg.at[at_z(-d)], at_z(-d), 2 * d, "all")
        lz(1, lg.at[at_z(-2)], at_z(-2), 2, "lo")
        lz(1, lg.at[at_z(2)], at_z(2), -2, "hi")
        for d in (-1, 1, -2, 2):
            twin_send(d)

    def lz_end():
        wait_bytes(lg.at[0:3], lz_recv.at[1])
        for d in (-3, 3, 4):
            twin_send(d)

    eye = ones_where(iota((128, 128), 0) == iota((128, 128), 1))

    def weights():
        fpf[...] = wz[...].astype(F32)
        for d in range(32):
            wd[32 * d : 32 * d + 32, :] = fpf[pl.ds(d, 32, stride=32), :].astype(BF16)
        wfull = dot_nt(eye, wd[...]).astype(BF16)
        wt[0:128, :] = wfull[:, 0:512]
        wt[128:256, :] = wfull[:, 512:1024]
        count = jnp.sum(sv4[...].astype(F32))
        inv = 1.0 / jnp.full((1, 128), count, F32)
        for i in range(48):
            scale[i : i + 1, :] = inv * rv_smem[gr * 48 + i].astype(F32)

    def turn_left():
        wait_bytes(lg.at[0:8], lt_recv)
        o2, i2 = iota((512, 1), 0), iota((512, 512), 1)
        perm2 = ones_where(((o2 // 2) % 16) * 32 + (o2 // 32) * 2 + o2 % 2 == i2)
        for b in range(3):
            x = jnp.concatenate([lg[:, 4 * b + e].reshape(512, 128).T for e in range(4)], axis=0)
            lt[512 * b : 512 * b + 512, :] = dot_nt(x, perm2).astype(BF16)

    half_lanes = iota((128, 128), 1) < 64

    off_a = pl.multiple_of(64 * core, 64)
    off_b = pl.multiple_of(128 - 128 * core, 64)

    def move_out(ib):
        rows = pl.ds(ib * 16, 16)
        return pltpu.make_async_copy(outv.at[rows], out_hbm.at[rows], out_sem.at[ib])

    def compute(k):
        t0 = PIECES[k]

        @pl.loop(0, 3)
        def _(ib):
            first_product(lt, rg, outer, ib, t0)
            at = t0 % 16 * 32
            if k < 2:
                w = wt[:, at : at + 256]
            else:
                w = wt[t0 // 16 * 128 : t0 // 16 * 128 + 128, at : at + 256]
            for i in range(0, 16, 2):
                y2 = second_product(w, outer, i)
                for e in range(2):
                    me = ib * 16 + i + e
                    y = y2[:, e * 128 : e * 128 + 128]
                    if k < 2:
                        y = jnp.where(half_lanes, y[0:128], y[128:256])
                    if k == 0:
                        accb[me] = y
                    elif k == 1:
                        y = (accb[me] + y).T
                        y = (y[0:64] + y[64:128]) * scale[pl.ds(me, 1), :] + bz[...]
                        outv[me, pl.ds(off_b, 64), :] = y.astype(BF16)
                    elif k == 2:
                        acc[me] = y
                    elif k < 5:
                        acc[me] = acc[me] + y
                    else:
                        y = (acc[me] + y).T * scale[pl.ds(me, 1), :] + bz[...]
                        outv[me, pl.ds(off_a, 128), :] = y.astype(BF16)
            if k == 5:
                move_out(ib).start()

    wait_bytes(rb.at[0, 0:15], rs_recv.at[0])
    assemble_right(0)
    wave(0)
    assemble_left()
    lz_start()
    wait_bytes(rb.at[1:3, 0:15], rs_recv.at[1])
    assemble_right(1)
    assemble_right(2)
    wave(1)
    wave(2)
    weights()
    wave(3)
    lz_forward()
    wave(4)
    lz_end()
    turn_left()
    compute(0)
    wave(5)
    compute(1)
    compute(2)
    wave(6)
    compute(3)
    wave(7)
    compute(4)
    wave(8)
    compute(5)

    wait_bytes(rg.at[0:15], g_send)
    wait_bytes(rb.at[:, 0:15], rs_send)
    wait_bytes(la.at[0:15], ls_send)
    wait_bytes(lg.at[0:7], lz_send)
    wait_bytes(lg.at[0:8], lt_send)

    @pl.loop(0, 3)
    def _(ib):
        move_out(ib).wait()


def hbm():
    return pl.BlockSpec(memory_space=pltpu.HBM)


def on_device(msa, sv, rv, gain, offset, w1, w2, wz, bz):
    dma = pltpu.SemaphoreType.DMA
    i32 = jnp.int32
    return pl.pallas_call(
        main_kernel,
        name="gather_and_compute",
        out_shape=jax.ShapeDtypeStruct((48, 192, 128), BF16),
        in_specs=[hbm()] * 11,
        out_specs=hbm(),
        scratch_shapes=[
            pltpu.VMEM((16, 48, 32, 128), BF16),
            pltpu.VMEM((1536, 512), BF16),
            pltpu.VMEM((48, 128, 128), F32),
            pltpu.VMEM((48, 128, 128), F32),
            pltpu.VMEM((48, 192, 128), BF16),
            pltpu.VMEM((48, 128), F32),
            pltpu.VMEM((256, 512), BF16),
            pltpu.VMEM((1, 128), F32),
            pltpu.SMEM((512,), i32),
            pltpu.SMEM((1536,), i32),
            pltpu.VMEM((4, 128), i32),
            pltpu.VMEM((12, 128), i32),
            pltpu.VMEM((2, 64, 1536), BF16),
            pltpu.VMEM((1, 64), F32),
            pltpu.VMEM((1, 64), F32),
            pltpu.VMEM((32, 64), BF16),
            pltpu.VMEM((32, 64), BF16),
            pltpu.VMEM((1024, 128), BF16),
            pltpu.VMEM((8, 3, 2, 16, 128), BF16),
            pltpu.VMEM((3, 16, 2, 16, 128), BF16),
            pltpu.VMEM((16, 48, 128), BF16),
            pltpu.VMEM((16, 48, 128), BF16),
            pltpu.VMEM((2, 12, 32, 128), BF16),
            pltpu.VMEM((16, 12, 32, 128), BF16),
            pltpu.VMEM((128, 1536), BF16),
            pltpu.VMEM((384, 512), BF16),
            pltpu.VMEM((2, 384, 128), F32),
            pltpu.VMEM((16, 48, 128), F32),
            pltpu.VMEM((8, 128), F32),
            pltpu.VMEM((1024, 128), F32),
            pltpu.VMEM((1024, 128), BF16),
            pltpu.VMEM((16, TILES, 32, 128), BF16),
            dma((11,)),
            dma((3,)),
            dma, dma((2,)),
            dma, dma,
            dma, dma((2,)),
            dma, dma,
            dma, dma((len(PIECES), 4)),
        ],
        compiler_params=pltpu.CompilerParams(
            collective_id=0, has_side_effects=True, vmem_limit_bytes=56 * 2**20),
    )(sv, sv.reshape(4, 128), rv, rv.reshape(12, 128), msa.transpose(0, 2, 1), gain.reshape(1, 64),
      offset.reshape(1, 64), w1.T, w2.T, wz, bz.reshape(1, 128))


def solution(mesh):
    in_specs = (P(("gr", "gc"), None, None), P(), P(), P(), P(), P(), P(), P(), P())
    out_specs = P("gr", "gc", None)
    return jax.shard_map(
        on_device, mesh=mesh, in_specs=in_specs, out_specs=out_specs, check_vma=False
    )
```

```python
import functools
import jax
import jax.numpy as jnp
from jax import lax
from jax.experimental import pallas as pl
from jax.experimental.pallas import tpu as pltpu
from jax.sharding import PartitionSpec as P

F32 = jnp.float32
BF16 = jnp.bfloat16
MESH = pl.DeviceIdType.MESH
NT = (((1,), (1,)), ((), ()))


def iota(shape, dim):
    return lax.broadcasted_iota(jnp.int32, shape, dim)


def ones_where(cond):
    return jnp.where(cond, 1.0, 0.0).astype(BF16)


def dot(a, b):
    return jnp.dot(a, b, preferred_element_type=F32)


def dot_nt(a, b):
    return lax.dot_general(a, b, NT, preferred_element_type=F32)


def where_am_i():
    gr = lax.axis_index("gr")
    gc = lax.axis_index("gc")
    zl = gr // 16
    pos = gr % 16
    zc = ((gc // 2) * 2 + zl) * 2 + gc % 2
    return gr, gc, zl, pos, zc


def ring_device(zl_to_gr, zc):
    z = zc // 2
    return {"gr": (z % 2) * 16 + zl_to_gr, "gc": (z // 2) * 2 + zc % 2}


def plane_device(zl, gc, pos):
    return {"gr": zl * 16 + pos, "gc": gc}


PIECES = ((32, 16), (0, 16), (16, 8), (24, 8))


def first_product(lt, rg, outer, ib, t0, n):
    x = lt[pl.ds(pl.multiple_of(ib * 512, 512), 512), :]
    for t in range(0, n, 2):
        w = jnp.concatenate([rg[:, t0 + t + e].reshape(512, 128) for e in range(2)], axis=1)
        s = dot(x, w).astype(BF16)
        for i in range(16):
            for e in range(2):
                outer[i, t + e] = s[i * 32 : i * 32 + 32, e * 128 : e * 128 + 128]


def second_product(w, outer, i, n):
    return dot(w, jnp.concatenate([outer[i + e, 0:n].reshape(n * 32, 128) for e in range(2)], axis=1))


def main_kernel(
    sv_hbm, sv4_hbm, rv_hbm, rv12_hbm, msa_hbm, gain_hbm, off_hbm, w1_hbm, w2_hbm, wz_hbm, bz_hbm,
    out_hbm,
    rg, lt, acc, outv, scale, wt, bz,
    sv_smem, rv_smem, sv4, rv12, msa, gain1, off1, w1, w2, wz,
    rs, rb, ls, la, lb, lg, n2, x4, lq, lsf, gainv, fpf, wd, outer,
    in_sem, out_sem, rs_send, rs_recv, ls_send, ls_recv, lz_send, lz_recv, lt_send, lt_recv,
    g_send, g_recv,
):
    gr, gc, zl, pos, zc = where_am_i()
    core = gc % 2
    px, py = pos // 4, pos % 4
    twin = {"gr": gr, "gc": gc + 1 - 2 * core}

    moves = [
        pltpu.make_async_copy(src, dst, in_sem.at[i])
        for i, (src, dst) in enumerate((
            (msa_hbm, msa), (gain_hbm, gain1), (off_hbm, off1), (w2_hbm, w2), (rv12_hbm, rv12), (sv_hbm, sv_smem),
            (w1_hbm, w1), (sv4_hbm, sv4), (rv_hbm, rv_smem), (wz_hbm, wz), (bz_hbm, bz)))
    ]
    for m in moves:
        m.start()

    barrier = pltpu.get_barrier_semaphore()

    @pl.loop(1, 16)
    def _(o):
        pl.semaphore_signal(barrier, inc=1, device_id=ring_device(pos, (zc + o) % 16), device_id_type=MESH)
        pl.semaphore_signal(barrier, inc=1, device_id=plane_device(zl, gc, (pos + o) % 16), device_id_type=MESH)

    for m in moves[:6]:
        m.wait()

    gainv[0:1, 0:64] = gain1[...]
    gainv[0:1, 64:128] = gain1[...]
    gainv[1:2, 0:64] = off1[...]
    gainv[1:2, 64:128] = off1[...]
    gcol = jnp.broadcast_to(gainv[0:1, :], (128, 128)).T[0:64]
    ocol = jnp.broadcast_to(gainv[1:2, :], (128, 128)).T[0:64]
    gcol = jnp.concatenate([gcol] * 3, axis=1)
    ocol = jnp.concatenate([ocol] * 3, axis=1)
    low = iota((16, 128), 1) < 64
    for g in range(4):
        present = jnp.concatenate([rv12[3 * g + k : 3 * g + k + 1, :] for k in range(3)], axis=1).astype(F32)
        for r in range(2):
            x = msa[r, :, 384 * g : 384 * g + 384].astype(F32)
            d = x - jnp.mean(x, axis=0, keepdims=True)
            var = jnp.mean(d * d, axis=0, keepdims=True)
            n = (d * lax.rsqrt(var + 1e-05) * gcol + ocol).astype(BF16)
            n2[r * 64 : r * 64 + 64, 384 * g : 384 * g + 384] = n
            yr = dot(w2[...], n) * (present * sv_smem[(gr * 8 + gc) * 2 + r].astype(F32))
            a, b = yr[0:16, 128:256], yr[16:32, 128:256]
            rs[2 * g, 0, r] = jnp.where(low, a, pltpu.roll(b, 64, axis=1)).astype(BF16)
            rs[2 * g, 1, r] = yr[0:16, 0:128].astype(BF16)
            rs[2 * g, 2, r] = yr[16:32, 0:128].astype(BF16)
            rs[2 * g + 1, 0, r] = jnp.where(low, pltpu.roll(a, 64, axis=1), b).astype(BF16)
            rs[2 * g + 1, 1, r] = yr[0:16, 256:384].astype(BF16)
            rs[2 * g + 1, 2, r] = yr[16:32, 256:384].astype(BF16)

    pl.semaphore_wait(barrier, 30)

    def wait_bytes(ref, sem):
        pltpu.make_async_copy(ref, ref, sem).wait()

    def rs_start(p):
        @pl.loop(1, 16)
        def _(o):
            to = ring_device(pos, (zc + o) % 16)
            pltpu.make_async_remote_copy(
                src_ref=rs.at[to["gc"], p], dst_ref=rb.at[p, zc],
                send_sem=rs_send, recv_sem=rs_recv.at[p],
                device_id=to, device_id_type=MESH).start()

        rb[p, zc] = rs[gc, p]

    rs_start(0)
    rs_start(1)

    for m in moves[6:]:
        m.wait()
    sel = ones_where((iota((128, 128), 0) % 32) * 4 + iota((128, 128), 0) // 32 == iota((128, 128), 1))
    for k in range(12):
        t = dot_nt(sel, n2[:, 128 * k : 128 * k + 128]).astype(BF16)
        for m in range(4):
            x4[32 * k : 32 * k + 32, 128 * m : 128 * m + 128] = t[32 * m : 32 * m + 32]
    t1 = ones_where(iota((512, 64), 0) % 64 == iota((512, 64), 1))
    t2 = ones_where(iota((32, 256), 1) % 32 == iota((32, 256), 0))
    row, col = iota((512, 256), 0), iota((512, 256), 1)
    wl = dot(dot_nt(t1, w1[...]).astype(BF16), t2)
    wl = jnp.where((row // 128 == (col // 32) % 4) & ((row // 64) % 2 == col // 128), wl, 0.0).astype(BF16)
    left = dot(x4[...], wl)
    lq[0] = left[:, 0:128]
    lq[1] = left[:, 128:256]
    for p in range(16):
        for l in range(2):
            for r in range(2):
                at = 12 * (l * 16 + p)
                lsf[p, l * 24 + r * 12 : l * 24 + r * 12 + 12, :] = lq[r, at : at + 12, :]
    ls[...] = lsf[...].astype(BF16)

    @pl.loop(1, 16)
    def _(o):
        to = (pos + o) % 16
        pltpu.make_async_remote_copy(
            src_ref=ls.at[to], dst_ref=la.at[pos],
            send_sem=ls_send, recv_sem=ls_recv,
            device_id=plane_device(zl, gc, to), device_id_type=MESH).start()

    la[pos] = ls[pos]

    def flat(x, y):
        return ((x + 4) % 4) * 4 + (y + 4) % 4

    def along(half, a, b):
        return flat(px + a, py + b) if half == 0 else flat(px + b, py + a)

    def g_send_to(k, half, level, who, part, da, db):
        t0, n = PIECES[k]
        unit = n // 2
        u0, un = {"both": (0, n), "all": (0, unit), "lo": (0, unit // 2), "hi": (unit // 2, unit // 2)}[part]
        t = pl.ds(t0 + unit * half + u0, un)
        pltpu.make_async_remote_copy(
            src_ref=rg.at[who, t], dst_ref=rg.at[who, t],
            send_sem=g_send, recv_sem=g_recv.at[k, level - 1],
            device_id=plane_device(zl, gc, along(half, da, db)), device_id_type=MESH).start()

    def both_ways(k, level, u):
        for h in range(2):
            g_send_to(k, h, level, along(h, u, 0), "all", 0, 1)
            g_send_to(k, h, level, along(h, u, 0), "all", 0, -1)

    def forward(k, u):
        for h in range(2):
            g_send_to(k, h, 4, along(h, u, -1), "lo", 0, 1)
            g_send_to(k, h, 4, along(h, u, 1), "hi", 0, -1)

    def level0(k):
        for da, db in ((1, 0), (-1, 0), (0, 1), (0, -1)):
            g_send_to(k, 0, 1, pos, "both", da, db)

    def level1(k):
        wait_bytes(rg.at[0:8, 0 : PIECES[k][1] // 2], g_recv.at[k, 0])
        for h in range(2):
            g_send_to(k, h, 2, along(h, -1, 0), "lo", 1, 0)
            g_send_to(k, h, 2, along(h, 1, 0), "hi", -1, 0)
        both_ways(k, 2, 3)
        both_ways(k, 2, 1)
        forward(k, 0)

    def level2(k):
        wait_bytes(rg.at[0:10, 0 : PIECES[k][1] // 2], g_recv.at[k, 1])
        both_ways(k, 3, 2)
        forward(k, 3)
        forward(k, 1)

    def level3(k):
        wait_bytes(rg.at[0:4, 0 : PIECES[k][1] // 2], g_recv.at[k, 2])
        forward(k, 2)

    def level4(k):
        wait_bytes(rg.at[0:8, 0 : PIECES[k][1] // 2], g_recv.at[k, 3])

    o0, i0 = iota((512, 1), 0), iota((512, 512), 1)
    perm0 = ones_where((o0 % 32) * 16 + o0 // 32 == i0)

    def assemble_right(p):
        wait_bytes(rb.at[p, 0:15], rs_recv.at[p])
        x = rb[p].reshape(512, 128)
        t0 = (32, 0, 16)[p]
        rg[pos, t0 : t0 + 16] = dot(perm0, x).astype(BF16).reshape(16, 32, 128)

    def assemble_left():
        o1, i1 = iota((768, 1), 0), iota((768, 768), 1)
        lq1 = o1 // 32
        l1 = jnp.where(lq1 >= 12, 1, 0)
        at = ((o1 // 2) % 16) * 48 + l1 * 24 + (o1 % 2) * 12 + (lq1 - 12 * l1)
        perm1 = ones_where(at == i1)

        wait_bytes(la.at[0:15], ls_recv)
        y = dot(perm1, la[...].reshape(768, 128)).astype(BF16)
        lb[...] = y.reshape(2, 12, 32, 128)
        lg[zc] = lb[zl]

    def at_z(d):
        return (zc + 2 * d + 16) % 16

    def lz(level, src, slot, to, part):
        t = pl.ds(*{"all": (0, 12), "lo": (0, 6), "hi": (6, 6)}[part])
        pltpu.make_async_remote_copy(
            src_ref=src.at[t], dst_ref=lg.at[slot, t],
            send_sem=lz_send, recv_sem=lz_recv.at[level],
            device_id=ring_device(pos, at_z(to)), device_id_type=MESH).start()

    def twin_send(d):
        pltpu.make_async_remote_copy(
            src_ref=lg.at[at_z(d)], dst_ref=lg.at[at_z(d)],
            send_sem=lt_send, recv_sem=lt_recv,
            device_id=twin, device_id_type=MESH).start()

    def lz_start():
        for d in (1, -1):
            lz(0, lb.at[1 - zl], zc, d, "all")
        for d in (2, -2):
            lz(0, lb.at[zl], zc, d, "all")
        twin_send(0)

    def lz_forward():
        wait_bytes(lg.at[0:4], lz_recv.at[0])
        for d in (1, -1):
            lz(1, lg.at[at_z(-d)], at_z(-d), 2 * d, "all")
        lz(1, lg.at[at_z(-2)], at_z(-2), 2, "lo")
        lz(1, lg.at[at_z(2)], at_z(2), -2, "hi")
        for d in (-1, 1, -2, 2):
            twin_send(d)

    def lz_end():
        wait_bytes(lg.at[0:3], lz_recv.at[1])
        for d in (-3, 3, 4):
            twin_send(d)

    eye = ones_where(iota((128, 128), 0) == iota((128, 128), 1))

    def weights():
        fpf[...] = wz[...].astype(F32)
        for d in range(32):
            wd[32 * d : 32 * d + 32, :] = fpf[pl.ds(d, 32, stride=32), :].astype(BF16)
        wfull = dot_nt(eye, wd[...]).astype(BF16)
        wt[0:128, :] = wfull[:, 0:512]
        wt[128:256, :] = wfull[:, 512:1024]
        count = jnp.sum(sv4[...].astype(F32))
        inv = 1.0 / jnp.full((1, 128), count, F32)
        for i in range(48):
            scale[i : i + 1, :] = inv * rv_smem[gr * 48 + i].astype(F32)

    def turn_left():
        wait_bytes(lg.at[0:8], lt_recv)
        o2, i2 = iota((512, 1), 0), iota((512, 512), 1)
        perm2 = ones_where(((o2 // 2) % 16) * 32 + (o2 // 32) * 2 + o2 % 2 == i2)
        for b in range(3):
            x = jnp.concatenate([lg[:, 4 * b + e].reshape(512, 128).T for e in range(4)], axis=0)
            lt[512 * b : 512 * b + 512, :] = dot_nt(x, perm2).astype(BF16)

    half_lanes = iota((128, 128), 1) < 64

    off_a = pl.multiple_of(64 * core, 64)
    off_b = pl.multiple_of(128 - 128 * core, 64)

    def move_out(ib):
        rows = pl.ds(ib * 16, 16)
        return pltpu.make_async_copy(outv.at[rows], out_hbm.at[rows], out_sem.at[ib])

    def compute(k, steps):
        t0, n = PIECES[k]

        @pl.loop(0, 3)
        def _(ib):
            for at, do in steps.items():
                pl.when(ib == at)(do)
            first_product(lt, rg, outer, ib, t0, n)
            if k == 0:
                w = wt[...]
            else:
                at = t0 % 16 * 32
                w = wt[t0 // 16 * 128 : t0 // 16 * 128 + 128, at : at + n * 32]
            for i in range(0, 16, 2):
                y2 = second_product(w, outer, i, n)
                for e in range(2):
                    me = ib * 16 + i + e
                    y = y2[:, e * 128 : e * 128 + 128]
                    if k == 0:
                        y = jnp.where(half_lanes, y[0:128], y[128:256]).T
                        y = (y[0:64] + y[64:128]) * scale[pl.ds(me, 1), :] + bz[...]
                        outv[me, pl.ds(off_b, 64), :] = y.astype(BF16)
                    elif k == 1:
                        acc[me] = y
                    elif k < 3:
                        acc[me] = acc[me] + y
                    else:
                        y = (acc[me] + y).T * scale[pl.ds(me, 1), :] + bz[...]
                        outv[me, pl.ds(off_a, 128), :] = y.astype(BF16)
            if k == 3:
                move_out(ib).start()

    assemble_right(0)
    level0(0)
    assemble_left()
    lz_start()
    rs_start(2)
    assemble_right(1)
    level0(1)
    level1(0)
    weights()
    level1(1)
    level2(0)
    lz_forward()
    level3(0)
    assemble_right(2)
    level0(2)
    level0(3)
    level2(1)
    level1(2)
    lz_end()
    level4(0)
    turn_left()
    level3(1)
    compute(0, {1: lambda: level1(3), 2: lambda: level2(2)})
    level4(1)
    level2(3)
    compute(1, {1: lambda: level3(2), 2: lambda: level3(3)})
    level4(2)
    compute(2, {})
    level4(3)
    compute(3, {})

    wait_bytes(rg.at[0:15], g_send)
    wait_bytes(rb.at[:, 0:15], rs_send)
    wait_bytes(la.at[0:15], ls_send)
    wait_bytes(lg.at[0:7], lz_send)
    wait_bytes(lg.at[0:8], lt_send)

    @pl.loop(0, 3)
    def _(ib):
        move_out(ib).wait()


def hbm():
    return pl.BlockSpec(memory_space=pltpu.HBM)


def on_device(msa, sv, rv, gain, offset, w1, w2, wz, bz):
    dma = pltpu.SemaphoreType.DMA
    i32 = jnp.int32
    return pl.pallas_call(
        main_kernel,
        name="gather_and_compute",
        out_shape=jax.ShapeDtypeStruct((48, 192, 128), BF16),
        in_specs=[hbm()] * 11,
        out_specs=hbm(),
        scratch_shapes=[
            pltpu.VMEM((16, 48, 32, 128), BF16),
            pltpu.VMEM((1536, 512), BF16),
            pltpu.VMEM((48, 128, 128), F32),
            pltpu.VMEM((48, 192, 128), BF16),
            pltpu.VMEM((48, 128), F32),
            pltpu.VMEM((256, 512), BF16),
            pltpu.VMEM((1, 128), F32),
            pltpu.SMEM((512,), i32),
            pltpu.SMEM((1536,), i32),
            pltpu.VMEM((4, 128), i32),
            pltpu.VMEM((12, 128), i32),
            pltpu.VMEM((2, 64, 1536), BF16),
            pltpu.VMEM((1, 64), F32),
            pltpu.VMEM((1, 64), F32),
            pltpu.VMEM((32, 64), BF16),
            pltpu.VMEM((32, 64), BF16),
            pltpu.VMEM((1024, 128), BF16),
            pltpu.VMEM((8, 3, 2, 16, 128), BF16),
            pltpu.VMEM((3, 16, 2, 16, 128), BF16),
            pltpu.VMEM((16, 48, 128), BF16),
            pltpu.VMEM((16, 48, 128), BF16),
            pltpu.VMEM((2, 12, 32, 128), BF16),
            pltpu.VMEM((16, 12, 32, 128), BF16),
            pltpu.VMEM((128, 1536), BF16),
            pltpu.VMEM((384, 512), BF16),
            pltpu.VMEM((2, 384, 128), F32),
            pltpu.VMEM((16, 48, 128), F32),
            pltpu.VMEM((8, 128), F32),
            pltpu.VMEM((1024, 128), F32),
            pltpu.VMEM((1024, 128), BF16),
            pltpu.VMEM((16, 16, 32, 128), BF16),
            dma((11,)),
            dma((3,)),
            dma, dma((3,)),
            dma, dma,
            dma, dma((2,)),
            dma, dma,
            dma, dma((len(PIECES), 4)),
        ],
        compiler_params=pltpu.CompilerParams(
            collective_id=0, has_side_effects=True, vmem_limit_bytes=56 * 2**20),
    )(sv, sv.reshape(4, 128), rv, rv.reshape(12, 128), msa.transpose(0, 2, 1), gain.reshape(1, 64),
      offset.reshape(1, 64), w1.T, w2.T, wz, bz.reshape(1, 128))


def solution(mesh):
    in_specs = (P(("gr", "gc"), None, None), P(), P(), P(), P(), P(), P(), P(), P())
    out_specs = P("gr", "gc", None)
    return jax.shard_map(
        on_device, mesh=mesh, in_specs=in_specs, out_specs=out_specs, check_vma=False
    )
```

```python
import functools
import jax
import jax.numpy as jnp
from jax import lax
from jax.experimental import pallas as pl
from jax.experimental.pallas import tpu as pltpu
from jax.sharding import PartitionSpec as P

F32 = jnp.float32
BF16 = jnp.bfloat16
MESH = pl.DeviceIdType.MESH
NT = (((1,), (1,)), ((), ()))


def iota(shape, dim):
    return lax.broadcasted_iota(jnp.int32, shape, dim)


def ones_where(cond):
    return jnp.where(cond, 1.0, 0.0).astype(BF16)


def dot(a, b):
    return jnp.dot(a, b, preferred_element_type=F32)


def dot_nt(a, b):
    return lax.dot_general(a, b, NT, preferred_element_type=F32)


def where_am_i():
    gr = lax.axis_index("gr")
    gc = lax.axis_index("gc")
    zl = gr // 16
    pos = gr % 16
    zc = ((gc // 2) * 2 + zl) * 2 + gc % 2
    return gr, gc, zl, pos, zc


def ring_device(zl_to_gr, zc):
    z = zc // 2
    return {"gr": (z % 2) * 16 + zl_to_gr, "gc": (z // 2) * 2 + zc % 2}


def plane_device(zl, gc, pos):
    return {"gr": zl * 16 + pos, "gc": gc}


ROWS = 24
PIECES = ((32, 16), (0, 16), (16, 8), (24, 8))


def first_product(lt, rg, outer, ib, t0, n):
    x = lt[pl.ds(pl.multiple_of(ib * ROWS * 32, ROWS * 32), ROWS * 32), :]
    for t in range(0, n, 2):
        w = jnp.concatenate([rg[:, t0 + t + e].reshape(512, 128) for e in range(2)], axis=1)
        s = dot(x, w).astype(BF16)
        for i in range(ROWS):
            for e in range(2):
                outer[i, t + e] = s[i * 32 : i * 32 + 32, e * 128 : e * 128 + 128]


def second_product(w, outer, i, n):
    return dot(w, jnp.concatenate([outer[i + e, 0:n].reshape(n * 32, 128) for e in range(2)], axis=1))


def main_kernel(
    sv_hbm, sv4_hbm, rv_hbm, rv12_hbm, msa_hbm, gain_hbm, off_hbm, w1_hbm, w2_hbm, wz_hbm, bz_hbm,
    out_hbm,
    rg, lt, acc, outv, scale, wt, bz,
    sv_smem, rv_smem, sv4, rv12, msa, gain1, off1, w1, w2, wz,
    rs, rb, ls, la, lb, lg, n2, x4, lq, lsf, gainv, fpf, wd, outer,
    in_sem, out_sem, rs_send, rs_recv, ls_send, ls_recv, lz_send, lz_recv, lt_send, lt_recv,
    g_send, g_recv,
):
    gr, gc, zl, pos, zc = where_am_i()
    core = gc % 2
    px, py = pos // 4, pos % 4
    twin = {"gr": gr, "gc": gc + 1 - 2 * core}

    moves = [
        pltpu.make_async_copy(src, dst, in_sem.at[i])
        for i, (src, dst) in enumerate((
            (msa_hbm, msa), (gain_hbm, gain1), (off_hbm, off1), (w2_hbm, w2), (rv12_hbm, rv12), (sv_hbm, sv_smem),
            (w1_hbm, w1), (sv4_hbm, sv4), (rv_hbm, rv_smem), (wz_hbm, wz), (bz_hbm, bz)))
    ]
    for m in moves:
        m.start()

    barrier = pltpu.get_barrier_semaphore()

    @pl.loop(1, 16)
    def _(o):
        pl.semaphore_signal(barrier, inc=1, device_id=ring_device(pos, (zc + o) % 16), device_id_type=MESH)
        pl.semaphore_signal(barrier, inc=1, device_id=plane_device(zl, gc, (pos + o) % 16), device_id_type=MESH)

    for m in moves[:6]:
        m.wait()

    gainv[0:1, 0:64] = gain1[...]
    gainv[0:1, 64:128] = gain1[...]
    gainv[1:2, 0:64] = off1[...]
    gainv[1:2, 64:128] = off1[...]
    gcol = jnp.broadcast_to(gainv[0:1, :], (128, 128)).T[0:64]
    ocol = jnp.broadcast_to(gainv[1:2, :], (128, 128)).T[0:64]
    gcol = jnp.concatenate([gcol] * 3, axis=1)
    ocol = jnp.concatenate([ocol] * 3, axis=1)
    low = iota((16, 128), 1) < 64
    for g in range(4):
        present = jnp.concatenate([rv12[3 * g + k : 3 * g + k + 1, :] for k in range(3)], axis=1).astype(F32)
        for r in range(2):
            x = msa[r, :, 384 * g : 384 * g + 384].astype(F32)
            d = x - jnp.mean(x, axis=0, keepdims=True)
            var = jnp.mean(d * d, axis=0, keepdims=True)
            n = (d * lax.rsqrt(var + 1e-05) * gcol + ocol).astype(BF16)
            n2[r * 64 : r * 64 + 64, 384 * g : 384 * g + 384] = n
            yr = dot(w2[...], n) * (present * sv_smem[(gr * 8 + gc) * 2 + r].astype(F32))
            a, b = yr[0:16, 128:256], yr[16:32, 128:256]
            rs[2 * g, 0, r] = jnp.where(low, a, pltpu.roll(b, 64, axis=1)).astype(BF16)
            rs[2 * g, 1, r] = yr[0:16, 0:128].astype(BF16)
            rs[2 * g, 2, r] = yr[16:32, 0:128].astype(BF16)
            rs[2 * g + 1, 0, r] = jnp.where(low, pltpu.roll(a, 64, axis=1), b).astype(BF16)
            rs[2 * g + 1, 1, r] = yr[0:16, 256:384].astype(BF16)
            rs[2 * g + 1, 2, r] = yr[16:32, 256:384].astype(BF16)

    pl.semaphore_wait(barrier, 30)

    def wait_bytes(ref, sem):
        pltpu.make_async_copy(ref, ref, sem).wait()

    def rs_start(p):
        @pl.loop(1, 16)
        def _(o):
            to = ring_device(pos, (zc + o) % 16)
            pltpu.make_async_remote_copy(
                src_ref=rs.at[to["gc"], p], dst_ref=rb.at[p, zc],
                send_sem=rs_send, recv_sem=rs_recv.at[p],
                device_id=to, device_id_type=MESH).start()

        rb[p, zc] = rs[gc, p]

    rs_start(0)
    rs_start(1)

    for m in moves[6:]:
        m.wait()
    sel = ones_where((iota((128, 128), 0) % 32) * 4 + iota((128, 128), 0) // 32 == iota((128, 128), 1))
    for k in range(12):
        t = dot_nt(sel, n2[:, 128 * k : 128 * k + 128]).astype(BF16)
        for m in range(4):
            x4[32 * k : 32 * k + 32, 128 * m : 128 * m + 128] = t[32 * m : 32 * m + 32]
    t1 = ones_where(iota((512, 64), 0) % 64 == iota((512, 64), 1))
    t2 = ones_where(iota((32, 256), 1) % 32 == iota((32, 256), 0))
    row, col = iota((512, 256), 0), iota((512, 256), 1)
    wl = dot(dot_nt(t1, w1[...]).astype(BF16), t2)
    wl = jnp.where((row // 128 == (col // 32) % 4) & ((row // 64) % 2 == col // 128), wl, 0.0).astype(BF16)
    left = dot(x4[...], wl)
    lq[0] = left[:, 0:128]
    lq[1] = left[:, 128:256]
    for p in range(16):
        for l in range(2):
            for r in range(2):
                at = 12 * (l * 16 + p)
                lsf[p, l * 24 + r * 12 : l * 24 + r * 12 + 12, :] = lq[r, at : at + 12, :]
    ls[...] = lsf[...].astype(BF16)

    @pl.loop(1, 16)
    def _(o):
        to = (pos + o) % 16
        pltpu.make_async_remote_copy(
            src_ref=ls.at[to], dst_ref=la.at[pos],
            send_sem=ls_send, recv_sem=ls_recv,
            device_id=plane_device(zl, gc, to), device_id_type=MESH).start()

    la[pos] = ls[pos]

    def flat(x, y):
        return ((x + 4) % 4) * 4 + (y + 4) % 4

    def along(half, a, b):
        return flat(px + a, py + b) if half == 0 else flat(px + b, py + a)

    def g_send_to(k, half, level, who, part, da, db):
        t0, n = PIECES[k]
        unit = n // 2
        u0, un = {"both": (0, n), "all": (0, unit), "lo": (0, unit // 2), "hi": (unit // 2, unit // 2)}[part]
        t = pl.ds(t0 + unit * half + u0, un)
        pltpu.make_async_remote_copy(
            src_ref=rg.at[who, t], dst_ref=rg.at[who, t],
            send_sem=g_send, recv_sem=g_recv.at[k, level - 1],
            device_id=plane_device(zl, gc, along(half, da, db)), device_id_type=MESH).start()

    def both_ways(k, level, u):
        for h in range(2):
            g_send_to(k, h, level, along(h, u, 0), "all", 0, 1)
            g_send_to(k, h, level, along(h, u, 0), "all", 0, -1)

    def forward(k, u):
        for h in range(2):
            g_send_to(k, h, 4, along(h, u, -1), "lo", 0, 1)
            g_send_to(k, h, 4, along(h, u, 1), "hi", 0, -1)

    def level0(k):
        for da, db in ((1, 0), (-1, 0), (0, 1), (0, -1)):
            g_send_to(k, 0, 1, pos, "both", da, db)

    def level1(k):
        wait_bytes(rg.at[0:8, 0 : PIECES[k][1] // 2], g_recv.at[k, 0])
        for h in range(2):
            g_send_to(k, h, 2, along(h, -1, 0), "lo", 1, 0)
            g_send_to(k, h, 2, along(h, 1, 0), "hi", -1, 0)
        both_ways(k, 2, 3)
        both_ways(k, 2, 1)
        forward(k, 0)

    def level2(k):
        wait_bytes(rg.at[0:10, 0 : PIECES[k][1] // 2], g_recv.at[k, 1])
        both_ways(k, 3, 2)
        forward(k, 3)
        forward(k, 1)

    def level3(k):
        wait_bytes(rg.at[0:4, 0 : PIECES[k][1] // 2], g_recv.at[k, 2])
        forward(k, 2)

    def level4(k):
        wait_bytes(rg.at[0:8, 0 : PIECES[k][1] // 2], g_recv.at[k, 3])

    o0, i0 = iota((512, 1), 0), iota((512, 512), 1)
    perm0 = ones_where((o0 % 32) * 16 + o0 // 32 == i0)

    def assemble_right(p):
        wait_bytes(rb.at[p, 0:15], rs_recv.at[p])
        x = rb[p].reshape(512, 128)
        t0 = (32, 0, 16)[p]
        rg[pos, t0 : t0 + 16] = dot(perm0, x).astype(BF16).reshape(16, 32, 128)

    def assemble_left():
        o1, i1 = iota((768, 1), 0), iota((768, 768), 1)
        lq1 = o1 // 32
        l1 = jnp.where(lq1 >= 12, 1, 0)
        at = ((o1 // 2) % 16) * 48 + l1 * 24 + (o1 % 2) * 12 + (lq1 - 12 * l1)
        perm1 = ones_where(at == i1)

        wait_bytes(la.at[0:15], ls_recv)
        y = dot(perm1, la[...].reshape(768, 128)).astype(BF16)
        lb[...] = y.reshape(2, 12, 32, 128)
        lg[zc] = lb[zl]

    def at_z(d):
        return (zc + 2 * d + 16) % 16

    def lz(level, src, slot, to, part):
        t = pl.ds(*{"all": (0, 12), "lo": (0, 6), "hi": (6, 6)}[part])
        pltpu.make_async_remote_copy(
            src_ref=src.at[t], dst_ref=lg.at[slot, t],
            send_sem=lz_send, recv_sem=lz_recv.at[level],
            device_id=ring_device(pos, at_z(to)), device_id_type=MESH).start()

    def twin_send(d):
        pltpu.make_async_remote_copy(
            src_ref=lg.at[at_z(d)], dst_ref=lg.at[at_z(d)],
            send_sem=lt_send, recv_sem=lt_recv,
            device_id=twin, device_id_type=MESH).start()

    def lz_start():
        for d in (1, -1):
            lz(0, lb.at[1 - zl], zc, d, "all")
        for d in (2, -2):
            lz(0, lb.at[zl], zc, d, "all")
        twin_send(0)

    def lz_forward():
        wait_bytes(lg.at[0:4], lz_recv.at[0])
        for d in (1, -1):
            lz(1, lg.at[at_z(-d)], at_z(-d), 2 * d, "all")
        lz(1, lg.at[at_z(-2)], at_z(-2), 2, "lo")
        lz(1, lg.at[at_z(2)], at_z(2), -2, "hi")
        for d in (-1, 1, -2, 2):
            twin_send(d)

    def lz_end():
        wait_bytes(lg.at[0:3], lz_recv.at[1])
        for d in (-3, 3, 4):
            twin_send(d)

    eye = ones_where(iota((128, 128), 0) == iota((128, 128), 1))

    def weights():
        fpf[...] = wz[...].astype(F32)
        for d in range(32):
            wd[32 * d : 32 * d + 32, :] = fpf[pl.ds(d, 32, stride=32), :].astype(BF16)
        wfull = dot_nt(eye, wd[...]).astype(BF16)
        wt[0:128, :] = wfull[:, 0:512]
        wt[128:256, :] = wfull[:, 512:1024]
        count = jnp.sum(sv4[...].astype(F32))
        inv = 1.0 / jnp.full((1, 128), count, F32)
        for i in range(48):
            scale[i : i + 1, :] = inv * rv_smem[gr * 48 + i].astype(F32)

    def turn_left():
        wait_bytes(lg.at[0:8], lt_recv)
        o2, i2 = iota((512, 1), 0), iota((512, 512), 1)
        perm2 = ones_where(((o2 // 2) % 16) * 32 + (o2 // 32) * 2 + o2 % 2 == i2)
        for b in range(3):
            x = jnp.concatenate([lg[:, 4 * b + e].reshape(512, 128).T for e in range(4)], axis=0)
            lt[512 * b : 512 * b + 512, :] = dot_nt(x, perm2).astype(BF16)

    half_lanes = iota((128, 128), 1) < 64

    off_a = pl.multiple_of(64 * core, 64)
    off_b = pl.multiple_of(128 - 128 * core, 64)

    def move_out(ib):
        rows = pl.ds(ib * ROWS, ROWS)
        return pltpu.make_async_copy(outv.at[rows], out_hbm.at[rows], out_sem.at[ib])

    def compute(k, steps):
        t0, n = PIECES[k]

        @pl.loop(0, 48 // ROWS)
        def _(ib):
            for at, do in steps.items():
                pl.when(ib == at)(do)
            first_product(lt, rg, outer, ib, t0, n)
            if k == 0:
                w = wt[...]
            else:
                at = t0 % 16 * 32
                w = wt[t0 // 16 * 128 : t0 // 16 * 128 + 128, at : at + n * 32]
            for i in range(0, ROWS, 2):
                y2 = second_product(w, outer, i, n)
                for e in range(2):
                    me = ib * ROWS + i + e
                    y = y2[:, e * 128 : e * 128 + 128]
                    if k == 0:
                        y = jnp.where(half_lanes, y[0:128], y[128:256]).T
                        y = (y[0:64] + y[64:128]) * scale[pl.ds(me, 1), :] + bz[...]
                        outv[me, pl.ds(off_b, 64), :] = y.astype(BF16)
                    elif k == 1:
                        acc[me] = y
                    elif k < 3:
                        acc[me] = acc[me] + y
                    else:
                        y = (acc[me] + y).T * scale[pl.ds(me, 1), :] + bz[...]
                        outv[me, pl.ds(off_a, 128), :] = y.astype(BF16)
            if k == 3:
                move_out(ib).start()

    assemble_right(0)
    level0(0)
    assemble_left()
    rs_start(2)
    lz_start()
    assemble_right(1)
    level0(1)
    level1(0)
    weights()
    level1(1)
    level2(0)
    assemble_right(2)
    level0(2)
    level0(3)
    lz_forward()
    level3(0)
    level2(1)
    level1(2)
    level1(3)
    lz_end()
    level4(0)
    turn_left()
    level3(1)

    def level2_both():
        level2(2)
        level2(3)

    compute(0, {1: level2_both})
    level4(1)
    level3(2)
    compute(1, {1: lambda: level3(3)})
    level4(2)
    compute(2, {})
    level4(3)
    compute(3, {})

    wait_bytes(rg.at[0:15], g_send)
    wait_bytes(rb.at[:, 0:15], rs_send)
    wait_bytes(la.at[0:15], ls_send)
    wait_bytes(lg.at[0:7], lz_send)
    wait_bytes(lg.at[0:8], lt_send)

    @pl.loop(0, 48 // ROWS)
    def _(ib):
        move_out(ib).wait()


def hbm():
    return pl.BlockSpec(memory_space=pltpu.HBM)


def on_device(msa, sv, rv, gain, offset, w1, w2, wz, bz):
    dma = pltpu.SemaphoreType.DMA
    i32 = jnp.int32
    return pl.pallas_call(
        main_kernel,
        name="gather_and_compute",
        out_shape=jax.ShapeDtypeStruct((48, 192, 128), BF16),
        in_specs=[hbm()] * 11,
        out_specs=hbm(),
        scratch_shapes=[
            pltpu.VMEM((16, 48, 32, 128), BF16),
            pltpu.VMEM((1536, 512), BF16),
            pltpu.VMEM((48, 128, 128), F32),
            pltpu.VMEM((48, 192, 128), BF16),
            pltpu.VMEM((48, 128), F32),
            pltpu.VMEM((256, 512), BF16),
            pltpu.VMEM((1, 128), F32),
            pltpu.SMEM((512,), i32),
            pltpu.SMEM((1536,), i32),
            pltpu.VMEM((4, 128), i32),
            pltpu.VMEM((12, 128), i32),
            pltpu.VMEM((2, 64, 1536), BF16),
            pltpu.VMEM((1, 64), F32),
            pltpu.VMEM((1, 64), F32),
            pltpu.VMEM((32, 64), BF16),
            pltpu.VMEM((32, 64), BF16),
            pltpu.VMEM((1024, 128), BF16),
            pltpu.VMEM((8, 3, 2, 16, 128), BF16),
            pltpu.VMEM((3, 16, 2, 16, 128), BF16),
            pltpu.VMEM((16, 48, 128), BF16),
            pltpu.VMEM((16, 48, 128), BF16),
            pltpu.VMEM((2, 12, 32, 128), BF16),
            pltpu.VMEM((16, 12, 32, 128), BF16),
            pltpu.VMEM((128, 1536), BF16),
            pltpu.VMEM((384, 512), BF16),
            pltpu.VMEM((2, 384, 128), F32),
            pltpu.VMEM((16, 48, 128), F32),
            pltpu.VMEM((8, 128), F32),
            pltpu.VMEM((1024, 128), F32),
            pltpu.VMEM((1024, 128), BF16),
            pltpu.VMEM((ROWS, 16, 32, 128), BF16),
            dma((11,)),
            dma((3,)),
            dma, dma((3,)),
            dma, dma,
            dma, dma((2,)),
            dma, dma,
            dma, dma((len(PIECES), 4)),
        ],
        compiler_params=pltpu.CompilerParams(
            collective_id=0, has_side_effects=True, vmem_limit_bytes=56 * 2**20),
    )(sv, sv.reshape(4, 128), rv, rv.reshape(12, 128), msa.transpose(0, 2, 1), gain.reshape(1, 64),
      offset.reshape(1, 64), w1.T, w2.T, wz, bz.reshape(1, 128))


def solution(mesh):
    in_specs = (P(("gr", "gc"), None, None), P(), P(), P(), P(), P(), P(), P(), P())
    out_specs = P("gr", "gc", None)
    return jax.shard_map(
        on_device, mesh=mesh, in_specs=in_specs, out_specs=out_specs, check_vma=False
    )
```
